32 devices in a mesh: frame: 8 (over y, x, core), row: 4 (over z).
Axes of the slice: x: 2, y: 2, z: 4, core: 2. Of those that a mesh axis runs over, the one named last changes fastest.
Arguments:
- query_raw: bfloat16 [8192, 1120], P(('frame', 'row')), may hold values from -6 to 6
- key_raw: bfloat16 [8192, 1120], P(('frame', 'row')), may hold values from -6 to 6
- values: bfloat16 [8192, 1120], P(('frame', 'row')), may hold values from -6 to 6
- norm_gain: float32 [1120], replicated, may hold values from 0.1 to 1.9
- grad_out: bfloat16 [8192, 1120], P(('frame', 'row')), may hold values from -6 to 6
Outputs:
- grad_query: bfloat16 [8192, 1120], P(('frame', 'row'))
- grad_key: bfloat16 [8192, 1120], P(('frame', 'row'))
- grad_value: bfloat16 [8192, 1120], P(('frame', 'row'))
The draws below stay inside these ranges and needn't reach their ends.
All inputs are finite; a program needn't handle non-finite values.
Results may differ from the reference program's by a relative error of at most 0.018.
Values may be sent and summed in bfloat16 or wider, within the bound.
A program may use at most 64 MiB of HBM per device.

```python
import jax
import jax.numpy as jnp
from jax import lax

HEADS = 10
HEAD_DIM = 112
TOK_DEV = 256
WIDTH = 1120
TOKENS = 8192
N_FRAME = 8
N_ROW = 4


def levels(rng, extent, cuts, smallest, largest):
    factor_of, own = 1.0, jax.random.fold_in(rng, 6)
    for position, shards_of in cuts:
        draws = jnp.exp(jax.random.uniform(jax.random.fold_in(own, position), (shards_of,), jnp.float32, smallest / len(cuts), largest / len(cuts)))
        factor_of = factor_of * jnp.repeat(draws, extent[position] // shards_of).reshape([-1 if axis == position else 1 for axis in range(len(extent))])
    return factor_of


def gaussian(key, extent, deviation, limit, split=(), dtype=jnp.bfloat16):
    entries = deviation * jax.random.normal(key, extent, jnp.float32)
    if split:
        entries = entries * levels(key, extent, split, -0.22, 0.18)
    return jnp.clip(entries, -limit, limit).astype(dtype)


def setup_inputs(seed: int = 0) -> dict:
    seeds = jax.random.split(jax.random.key(seed), 6)
    query_raw = gaussian(seeds[0], (TOKENS, WIDTH), 1.0, 6.0, ((0, 32),))
    key_raw = gaussian(seeds[1], (TOKENS, WIDTH), 1.0, 6.0, ((0, 32),))
    values = gaussian(seeds[2], (TOKENS, WIDTH), 1.0, 6.0, ((0, 32),))
    norm_gain = jnp.clip(1.0 + 0.18 * jax.random.normal(seeds[3], (WIDTH,), jnp.float32), 0.1, 1.9)
    grad_out = gaussian(seeds[4], (TOKENS, WIDTH), 1.0, 6.0, ((0, 32),))
    return {"query_raw": query_raw, "key_raw": key_raw, "values": values, "norm_gain": norm_gain, "grad_out": grad_out}


def feature(raw_values):
    return jnp.where(raw_values > 0, raw_values + 1.0, jnp.exp(jnp.minimum(raw_values, 0.0)))

def slope_of(raw_values):
    return jnp.where(raw_values > 0, 1.0, jnp.exp(jnp.minimum(raw_values, 0.0)))

def reference(query_raw, key_raw, values, norm_gain, grad_out):
    block_rows = TOK_DEV * N_ROW
    split_shape = (N_FRAME, block_rows, HEADS, HEAD_DIM)
    query_blocks = query_raw.reshape(split_shape)
    key_blocks = key_raw.reshape(split_shape)
    value_blocks = values.reshape(split_shape)
    grad_blocks = grad_out.reshape(split_shape)
    gain_heads = norm_gain.reshape(HEADS, HEAD_DIM).astype(jnp.float32)

    def block_state(pair):
        key_block, value_block = pair
        key_feat = feature(key_block.astype(jnp.float32)).astype(jnp.bfloat16)
        return jnp.einsum('thi,thj->hij', key_feat.astype(jnp.float32), value_block.astype(jnp.float32))
    states = lax.map(block_state, (key_blocks, value_blocks))
    prefix = jnp.cumsum(states, axis=0).astype(jnp.bfloat16)

    def query_side(triple):
        query_block, grad_block, prefix_block = triple
        query_float = query_block.astype(jnp.float32)
        query_feat = feature(query_float).astype(jnp.bfloat16)
        prefix_float = prefix_block.astype(jnp.float32)
        attention = jnp.einsum('thi,hij->thj', query_feat.astype(jnp.float32), prefix_float)
        mean_square = lax.optimization_barrier(jnp.mean(attention * attention, axis=-1, keepdims=True))
        inv_rms = lax.rsqrt(mean_square + 1e-06)
        weighted = grad_block.astype(jnp.float32) * gain_heads
        inner = lax.optimization_barrier(jnp.mean(weighted * attention, axis=-1, keepdims=True))
        grad_attention = (inv_rms * weighted - attention * inv_rms * inv_rms * inv_rms * inner).astype(jnp.bfloat16)
        grad_feat = jnp.einsum('thj,hij->thi', grad_attention.astype(jnp.float32), prefix_float)
        grad_q = (grad_feat * slope_of(query_float)).astype(jnp.bfloat16)
        adjoint_term = jnp.einsum('thi,thj->hij', query_feat.astype(jnp.float32), grad_attention.astype(jnp.float32))
        return (grad_q, adjoint_term)
    grad_q, adjoint_terms = lax.map(query_side, (query_blocks, grad_blocks, prefix))
    adjoint = jnp.flip(jnp.cumsum(jnp.flip(adjoint_terms, 0), axis=0), 0).astype(jnp.bfloat16)

    def key_side(triple):
        key_block, value_block, adjoint_block = triple
        key_float = key_block.astype(jnp.float32)
        key_feat = feature(key_float).astype(jnp.bfloat16)
        adjoint_float = adjoint_block.astype(jnp.float32)
        grad_v = jnp.einsum('thi,hij->thj', key_feat.astype(jnp.float32), adjoint_float).astype(jnp.bfloat16)
        grad_feat = jnp.einsum('thj,hij->thi', value_block.astype(jnp.float32), adjoint_float)
        grad_k = (grad_feat * slope_of(key_float)).astype(jnp.bfloat16)
        return (grad_k, grad_v)
    grad_k, grad_v = lax.map(key_side, (key_blocks, value_blocks, adjoint))
    flat_shape = (TOKENS, HEADS * HEAD_DIM)
    return (grad_q.reshape(flat_shape), grad_k.reshape(flat_shape), grad_v.reshape(flat_shape))
```

```python
import functools

import jax
import jax.numpy as jnp
from jax import lax
from jax.experimental import pallas as pl
from jax.experimental.pallas import tpu as pltpu
from jax.sharding import PartitionSpec as P

HEAD_DIM = 112
LANES = 128
MESH = pl.DeviceIdType.MESH
TN = (((0,), (0,)), ((), ()))
NT = (((1,), (1,)), ((), ()))
NN = (((1,), (0,)), ((), ()))


def dot(a, b, dims):
    return lax.dot_general(a, b, dims, preferred_element_type=jnp.float32)


def kernel(groups, piece, rows_n, frames_n, q_hbm, k_hbm, v_hbm, gain_ref, g_hbm,
           gq_hbm, gk_hbm, gv_hbm,
           q_raw, k_raw, v_raw, g_raw, gq_out, gk_out, gv_out,
           q_feat, k_feat, v_head, q_slope, k_slope, weighted, grad_att,
           send_buf, rs_buf, share, fr_send, fr_buf, ag_send, whole,
           in_sem, out_sem, rs_ssem, rs_rsem, fr_ssem, fr_rsem, ag_ssem, ag_rsem):
    D = HEAD_DIM
    owners = 2 * rows_n
    chips = frames_n // 2
    frame, row = lax.axis_index("frame"), lax.axis_index("row")
    chip, core = frame // 2, frame % 2
    me = row * 2 + core

    def column_id(step):
        dest = lax.rem(me + step, owners)
        return (chip * 2 + dest % 2, dest // 2)

    def chip_id(step):
        return (lax.rem(chip + step, chips) * 2 + core, row)

    loads = [
        pltpu.make_async_copy(src, dst, in_sem.at[i])
        for i, (src, dst) in enumerate(
            [(k_hbm, k_raw), (v_hbm, v_raw), (q_hbm, q_raw), (g_hbm, g_raw)])
    ]
    for c in loads:
        c.start()

    barrier = pltpu.get_barrier_semaphore()
    for j in range(1, owners):
        pl.semaphore_signal(barrier, inc=1, device_id=column_id(j), device_id_type=MESH)
    for j in range(1, chips):
        pl.semaphore_signal(barrier, inc=1, device_id=chip_id(j), device_id_type=MESH)

    def cols(h):
        return slice(h * D, (h + 1) * D)

    def phi(raw):
        low = jnp.exp(jnp.minimum(raw, 0.0))
        return jnp.where(raw > 0, raw + 1.0, low), jnp.where(raw > 0, 1.0, low)

    def rs_copy(p, g, j):
        dest = lax.rem(me + j, owners)
        return pltpu.make_async_remote_copy(
            src_ref=send_buf.at[p, g, pl.ds(pl.multiple_of(dest * piece, 16), piece)],
            dst_ref=rs_buf.at[p, g, j],
            send_sem=rs_ssem.at[p, g, j], recv_sem=rs_rsem.at[p, g, j],
            device_id=column_id(j), device_id_type=MESH)

    def fr_copy(p, g, j):
        return pltpu.make_async_remote_copy(
            src_ref=fr_send.at[p, g], dst_ref=fr_buf.at[p, g, j],
            send_sem=fr_ssem.at[p, g, j], recv_sem=fr_rsem.at[p, g, j],
            device_id=chip_id(j), device_id_type=MESH)

    def ag_copy(p, g, j):
        return pltpu.make_async_remote_copy(
            src_ref=ag_send.at[p, g, j % 2],
            dst_ref=whole.at[p, g, pl.ds(pl.multiple_of(me * piece, 16), piece)],
            send_sem=ag_ssem.at[p, g, j], recv_sem=ag_rsem.at[p, g, j],
            device_id=column_id(j), device_id_type=MESH)

    def ag_wait(p, g, j):
        src = lax.rem(me - j + owners, owners)
        pltpu.make_async_remote_copy(
            src_ref=ag_send.at[p, g, j % 2],
            dst_ref=whole.at[p, g, pl.ds(pl.multiple_of(src * piece, 16), piece)],
            send_sem=ag_ssem.at[p, g, j], recv_sem=ag_rsem.at[p, g, j],
            device_id=column_id(j), device_id_type=MESH).wait_recv()

    def start_rs(p, g):
        for j in range(1, owners):
            rs_copy(p, g, j).start()

    def reduce_rows(p, g):
        own = pl.ds(pl.multiple_of(me * piece, 16), piece)
        mine = send_buf[p, g, own, :].astype(jnp.float32)
        other = None
        for j in range(1, owners):
            rs_copy(p, g, j).wait_recv()
        for j in range(1, owners):
            block = rs_buf[p, g, j].astype(jnp.float32)
            if j % 2 == 0:
                mine = mine + block
            else:
                other = block if other is None else other + block
        share[p, g, 0] = mine
        share[p, g, 1] = other
        fr_send[p, g] = (mine + other).astype(jnp.bfloat16)
        for j in range(1, chips):
            fr_copy(p, g, j).start()

    def scan_frames(p, g):
        for j in range(1, chips):
            fr_copy(p, g, j).wait_recv()
        base = jnp.zeros((piece, LANES), jnp.float32)
        for j in range(1, chips):
            keep = (j <= chip) if p == 0 else (j > chip)
            base = base + jnp.where(keep, fr_buf[p, g, j].astype(jnp.float32), 0.0)
        mine, other = share[p, g, 0], share[p, g, 1]
        own_last = (core == 1) if p == 0 else (core == 0)
        ag_send[p, g, 0] = (base + mine + jnp.where(own_last, other, 0.0)).astype(jnp.bfloat16)
        ag_send[p, g, 1] = (base + other + jnp.where(own_last, 0.0, mine)).astype(jnp.bfloat16)
        for j in range(1, owners):
            ag_copy(p, g, j).start()
        own = pl.ds(pl.multiple_of(me * piece, 16), piece)
        whole[p, g, own, :] = ag_send[p, g, 0]

    def wait_whole(p, g):
        for j in range(1, owners):
            ag_wait(p, g, j)

    span = range(len(groups))

    def head_state(p, g, i):
        return whole[p, g, i * D:(i + 1) * D, :D]

    loads[0].wait()
    loads[1].wait()
    for g in span:
        for i, h in enumerate(groups[g]):
            feat, slope = phi(k_raw[:, cols(h)].astype(jnp.float32))
            feat = feat.astype(jnp.bfloat16)
            val = v_raw[:, cols(h)]
            k_feat[h] = feat
            k_slope[h] = slope
            v_head[h] = val
            send_buf[0, g, i * D:(i + 1) * D, :D] = dot(feat, val, TN).astype(jnp.bfloat16)
        if g == 0:
            pl.semaphore_wait(barrier, owners - 1 + chips - 1)
        start_rs(0, g)

    loads[2].wait()
    loads[3].wait()
    for g in span:
        for h in groups[g]:
            feat, slope = phi(q_raw[:, cols(h)].astype(jnp.float32))
            q_feat[h] = feat.astype(jnp.bfloat16)
            q_slope[h] = slope
            weighted[h] = g_raw[:, cols(h)].astype(jnp.float32) * gain_ref[:, cols(h)]

    for g in span:
        reduce_rows(0, g)
    for g in span:
        scan_frames(0, g)

    for g in span:
        wait_whole(0, g)
        for i, h in enumerate(groups[g]):
            att = dot(q_feat[h], head_state(0, g, i), NN)
            w = weighted[h]
            inv = lax.rsqrt(jnp.mean(att * att, axis=-1, keepdims=True) + 1e-6)
            inner = jnp.mean(w * att, axis=-1, keepdims=True)
            ga = (inv * w - att * (inv * inv * inv * inner)).astype(jnp.bfloat16)
            grad_att[h] = ga
            send_buf[1, g, i * D:(i + 1) * D, :D] = dot(q_feat[h], ga, TN).astype(jnp.bfloat16)
        start_rs(1, g)

    for g in span:
        for i, h in enumerate(groups[g]):
            gq = dot(grad_att[h], head_state(0, g, i), NT) * q_slope[h]
            gq_out[:, cols(h)] = gq.astype(jnp.bfloat16)
    stores = [
        pltpu.make_async_copy(src, dst, out_sem.at[i])
        for i, (src, dst) in enumerate([(gq_out, gq_hbm), (gk_out, gk_hbm), (gv_out, gv_hbm)])
    ]
    stores[0].start()

    for g in span:
        reduce_rows(1, g)
    for g in span:
        scan_frames(1, g)
    for g in span:
        wait_whole(1, g)
        for i, h in enumerate(groups[g]):
            adj = head_state(1, g, i)
            gv_out[:, cols(h)] = dot(k_feat[h], adj, NN).astype(jnp.bfloat16)
            gk_out[:, cols(h)] = (dot(v_head[h], adj, NT) * k_slope[h]).astype(jnp.bfloat16)
    stores[1].start()
    stores[2].start()

    for p in range(2):
        for g in span:
            for j in range(1, owners):
                rs_copy(p, g, j).wait_send()
                ag_copy(p, g, j).wait_send()
            for j in range(1, chips):
                fr_copy(p, g, j).wait_send()
    for c in stores:
        c.wait()


GROUPS = 2


def body(rows_n, frames_n, query_raw, key_raw, values, norm_gain, grad_out):
    tok, width = query_raw.shape
    heads = width // HEAD_DIM
    owners, chips = 2 * rows_n, frames_n // 2
    size = -(-heads // GROUPS)
    groups = [list(range(s, min(s + size, heads))) for s in range(0, heads, size)]
    n = len(groups)
    unit = 16 * owners
    piece = -(-size * HEAD_DIM // unit) * 16
    bf, f32 = jnp.bfloat16, jnp.float32
    raw = pltpu.VMEM((tok, width), bf)
    per_head = lambda t: pltpu.VMEM((heads, tok, HEAD_DIM), t)
    dma = pltpu.SemaphoreType.DMA
    out = jax.ShapeDtypeStruct((tok, width), bf)
    flops = 12 * tok * heads * HEAD_DIM * HEAD_DIM
    hbm = pl.BlockSpec(memory_space=pl.ANY)
    return pl.pallas_call(
        functools.partial(kernel, groups, piece, rows_n, frames_n),
        out_shape=(out, out, out),
        in_specs=[hbm, hbm, hbm, pl.BlockSpec(memory_space=pltpu.VMEM), hbm],
        out_specs=(hbm, hbm, hbm),
        scratch_shapes=[
            raw, raw, raw, raw, raw, raw, raw,
            per_head(bf), per_head(bf), per_head(bf), per_head(f32), per_head(f32),
            per_head(f32), per_head(bf),
            pltpu.VMEM((2, n, owners * piece, LANES), bf),
            pltpu.VMEM((2, n, owners, piece, LANES), bf),
            pltpu.VMEM((2, n, 2, piece, LANES), f32),
            pltpu.VMEM((2, n, piece, LANES), bf),
            pltpu.VMEM((2, n, chips, piece, LANES), bf),
            pltpu.VMEM((2, n, 2, piece, LANES), bf),
            pltpu.VMEM((2, n, owners * piece, LANES), bf),
            dma((4,)), dma((3,)),
            dma((2, n, owners)), dma((2, n, owners)),
            dma((2, n, chips)), dma((2, n, chips)),
            dma((2, n, owners)), dma((2, n, owners)),
        ],
        cost_estimate=pl.CostEstimate(
            flops=flops, bytes_accessed=14 * tok * width, transcendentals=2 * tok * width),
        compiler_params=pltpu.CompilerParams(
            collective_id=0, has_side_effects=True, vmem_limit_bytes=48 * 1024 * 1024),
    )(query_raw, key_raw, values, norm_gain.reshape(1, width), grad_out)


def solution(mesh):
    split = P(("frame", "row"), None)
    return jax.shard_map(
        functools.partial(body, mesh.shape["row"], mesh.shape["frame"]),
        mesh=mesh,
        in_specs=(split, split, split, P(), split),
        out_specs=(split, split, split),
        check_vma=False,
    )
```

```python
import functools

import jax
import jax.numpy as jnp
from jax import lax
from jax.experimental import pallas as pl
from jax.experimental.pallas import tpu as pltpu
from jax.sharding import PartitionSpec as P

HEAD_DIM = 112
LANES = 128
MESH = pl.DeviceIdType.MESH
TN = (((0,), (0,)), ((), ()))
NT = (((1,), (1,)), ((), ()))
NN = (((1,), (0,)), ((), ()))


def dot(a, b, dims):
    return lax.dot_general(a, b, dims, preferred_element_type=jnp.float32)


def kernel(groups, pieces, rows_n, frames_n, q_hbm, k_hbm, v_hbm, gain_ref, g_hbm,
           gq_hbm, gk_hbm, gv_hbm,
           q_raw, k_raw, v_raw, g_raw, gq_out, gk_out, gv_out,
           q_feat, k_feat, gain, q_slope, k_slope, weighted, grad_att,
           send_buf, rs_buf, share, fr_send, fr_buf, ag_send, whole,
           in_sem, out_sem, rs_ssem, rs_rsem, fr_ssem, fr_rsem, ag_ssem, ag_rsem):
    D = HEAD_DIM
    owners = 2 * rows_n
    chips = frames_n // 2
    frame, row = lax.axis_index("frame"), lax.axis_index("row")
    chip, core = frame // 2, frame % 2
    me = row * 2 + core

    def column_id(step):
        dest = lax.rem(me + step, owners)
        return (chip * 2 + dest % 2, dest // 2)

    def chip_id(step):
        return (lax.rem(chip + step, chips) * 2 + core, row)

    loads = [
        pltpu.make_async_copy(src, dst, in_sem.at[i])
        for i, (src, dst) in enumerate(
            [(k_hbm, k_raw), (v_hbm, v_raw), (q_hbm, q_raw), (g_hbm, g_raw)])
    ]
    for c in loads:
        c.start()

    barrier = pltpu.get_barrier_semaphore()
    for j in range(1, owners):
        pl.semaphore_signal(barrier, inc=1, device_id=column_id(j), device_id_type=MESH)
    for j in range(1, chips):
        pl.semaphore_signal(barrier, inc=1, device_id=chip_id(j), device_id_type=MESH)

    def cols(h):
        return slice(h * D, (h + 1) * D)

    base_of = [sum(pieces[:g]) * owners for g in range(len(groups))]
    slot_of = [sum(pieces[:g]) for g in range(len(groups))]

    def rows_of(g, index):
        return pl.ds(pl.multiple_of(base_of[g] + index * pieces[g], 16), pieces[g])

    def slot(g):
        return pl.ds(slot_of[g], pieces[g])

    def phi(raw):
        low = jnp.exp(jnp.minimum(raw, 0.0))
        return jnp.where(raw > 0, raw + 1.0, low), jnp.where(raw > 0, 1.0, low)

    def rs_copy(p, g, j):
        dest = lax.rem(me + j, owners)
        return pltpu.make_async_remote_copy(
            src_ref=send_buf.at[p, rows_of(g, dest)],
            dst_ref=rs_buf.at[p, j, slot(g)],
            send_sem=rs_ssem.at[p, g, j], recv_sem=rs_rsem.at[p, g, j],
            device_id=column_id(j), device_id_type=MESH)

    def fr_copy(p, g, j):
        return pltpu.make_async_remote_copy(
            src_ref=fr_send.at[p, slot(g)], dst_ref=fr_buf.at[p, j, slot(g)],
            send_sem=fr_ssem.at[p, g, j], recv_sem=fr_rsem.at[p, g, j],
            device_id=chip_id(j), device_id_type=MESH)

    def ag_copy(p, g, j):
        return pltpu.make_async_remote_copy(
            src_ref=ag_send.at[p, j % 2, slot(g)],
            dst_ref=whole.at[p, rows_of(g, me)],
            send_sem=ag_ssem.at[p, g, j], recv_sem=ag_rsem.at[p, g, j],
            device_id=column_id(j), device_id_type=MESH)

    def ag_wait(p, g, j):
        src = lax.rem(me - j + owners, owners)
        pltpu.make_async_remote_copy(
            src_ref=ag_send.at[p, j % 2, slot(g)],
            dst_ref=whole.at[p, rows_of(g, src)],
            send_sem=ag_ssem.at[p, g, j], recv_sem=ag_rsem.at[p, g, j],
            device_id=column_id(j), device_id_type=MESH).wait_recv()

    def start_rs(p, g):
        for j in range(1, owners):
            rs_copy(p, g, j).start()

    def reduce_rows(p, g):
        mine = send_buf[p, rows_of(g, me), :].astype(jnp.float32)
        other = None
        for j in range(1, owners):
            rs_copy(p, g, j).wait_recv()
        for j in range(1, owners):
            block = rs_buf[p, j, slot(g), :].astype(jnp.float32)
            if j % 2 == 0:
                mine = mine + block
            else:
                other = block if other is None else other + block
        share[p, 0, slot(g), :] = mine
        share[p, 1, slot(g), :] = other
        fr_send[p, slot(g), :] = (mine + other).astype(jnp.bfloat16)
        for j in range(1, chips):
            fr_copy(p, g, j).start()

    def scan_frames(p, g):
        for j in range(1, chips):
            fr_copy(p, g, j).wait_recv()
        base = jnp.zeros((pieces[g], LANES), jnp.float32)
        for j in range(1, chips):
            keep = (j <= chip) if p == 0 else (j > chip)
            base = base + jnp.where(keep, fr_buf[p, j, slot(g), :].astype(jnp.float32), 0.0)
        mine, other = share[p, 0, slot(g), :], share[p, 1, slot(g), :]
        own_last = (core == 1) if p == 0 else (core == 0)
        ag_send[p, 0, slot(g), :] = (base + mine + jnp.where(own_last, other, 0.0)).astype(jnp.bfloat16)
        ag_send[p, 1, slot(g), :] = (base + other + jnp.where(own_last, 0.0, mine)).astype(jnp.bfloat16)
        for j in range(1, owners):
            ag_copy(p, g, j).start()
        whole[p, rows_of(g, me), :] = ag_send[p, 0, slot(g), :]

    def wait_whole(p, g):
        for j in range(1, owners):
            ag_wait(p, g, j)

    span = range(len(groups))

    def head_state(p, g, i):
        return whole[p, base_of[g] + i * D:base_of[g] + (i + 1) * D, :D]

    loads[0].wait()
    loads[1].wait()
    for g in span:
        for i, h in enumerate(groups[g]):
            feat, slope = phi(k_raw[cols(h), :].astype(jnp.float32))
            feat = feat.astype(jnp.bfloat16)
            val = v_raw[cols(h), :]
            k_feat[h] = feat
            k_slope[h] = slope
            send_buf[0, base_of[g] + i * D:base_of[g] + (i + 1) * D, :D] = dot(feat, val, NT).astype(jnp.bfloat16)
        if g == 0:
            pl.semaphore_wait(barrier, owners - 1 + chips - 1)
        start_rs(0, g)

    loads[2].wait()
    loads[3].wait()
    tok, width = q_raw.shape[1], q_raw.shape[0]
    gain[...] = jnp.broadcast_to(gain_ref[...].reshape(1, width), (tok, width)).T
    for g in span:
        for h in groups[g]:
            feat, slope = phi(q_raw[cols(h), :].astype(jnp.float32))
            q_feat[h] = feat.astype(jnp.bfloat16)
            q_slope[h] = slope
            weighted[h] = g_raw[cols(h), :].astype(jnp.float32) * gain[cols(h), :]

    for g in span:
        reduce_rows(0, g)
    for g in span:
        scan_frames(0, g)

    for g in span:
        wait_whole(0, g)
        for i, h in enumerate(groups[g]):
            att = dot(head_state(0, g, i), q_feat[h], TN)
            w = weighted[h]
            inv = lax.rsqrt(jnp.mean(att * att, axis=0, keepdims=True) + 1e-6)
            inner = jnp.mean(w * att, axis=0, keepdims=True)
            ga = (inv * w - att * (inv * inv * inv * inner)).astype(jnp.bfloat16)
            grad_att[h] = ga
            send_buf[1, base_of[g] + i * D:base_of[g] + (i + 1) * D, :D] = dot(q_feat[h], ga, NT).astype(jnp.bfloat16)
        start_rs(1, g)

    for g in span:
        for i, h in enumerate(groups[g]):
            gq = dot(head_state(0, g, i), grad_att[h], NN) * q_slope[h]
            gq_out[cols(h), :] = gq.astype(jnp.bfloat16)
    stores = [
        pltpu.make_async_copy(src, dst, out_sem.at[i])
        for i, (src, dst) in enumerate([(gq_out, gq_hbm), (gk_out, gk_hbm), (gv_out, gv_hbm)])
    ]
    stores[0].start()

    for g in span:
        reduce_rows(1, g)
    for g in span:
        scan_frames(1, g)
    for g in span:
        wait_whole(1, g)
        for i, h in enumerate(groups[g]):
            adj = head_state(1, g, i)
            gv_out[cols(h), :] = dot(adj, k_feat[h], TN).astype(jnp.bfloat16)
            gk_out[cols(h), :] = (dot(adj, v_raw[cols(h), :], NN) * k_slope[h]).astype(jnp.bfloat16)
    stores[1].start()
    stores[2].start()

    for p in range(2):
        for g in span:
            for j in range(1, owners):
                rs_copy(p, g, j).wait_send()
                ag_copy(p, g, j).wait_send()
            for j in range(1, chips):
                fr_copy(p, g, j).wait_send()
    for c in stores:
        c.wait()


def body(rows_n, frames_n, query_raw, key_raw, values, norm_gain, grad_out):
    tok, width = query_raw.shape
    heads = width // HEAD_DIM
    owners, chips = 2 * rows_n, frames_n // 2
    first = max(1, heads * 4 // 5)
    groups = [g for g in (list(range(first)), list(range(first, heads))) if g]
    n = len(groups)
    unit = 16 * owners
    pieces = [-(-len(g) * HEAD_DIM // unit) * 16 for g in groups]
    piece = sum(pieces)
    bf, f32 = jnp.bfloat16, jnp.float32
    raw = pltpu.VMEM((width, tok), bf)
    per_head = lambda t: pltpu.VMEM((heads, HEAD_DIM, tok), t)
    dma = pltpu.SemaphoreType.DMA
    out = jax.ShapeDtypeStruct((width, tok), bf)
    flops = 12 * tok * heads * HEAD_DIM * HEAD_DIM
    hbm = pl.BlockSpec(memory_space=pl.ANY)
    grads = pl.pallas_call(
        functools.partial(kernel, groups, pieces, rows_n, frames_n),
        out_shape=(out, out, out),
        in_specs=[hbm, hbm, hbm, pl.BlockSpec(memory_space=pltpu.VMEM), hbm],
        out_specs=(hbm, hbm, hbm),
        scratch_shapes=[
            raw, raw, raw, raw, raw, raw, raw,
            per_head(bf), per_head(bf), pltpu.VMEM((width, tok), f32),
            per_head(f32), per_head(f32), per_head(f32), per_head(bf),
            pltpu.VMEM((2, owners * piece, LANES), bf),
            pltpu.VMEM((2, owners, piece, LANES), bf),
            pltpu.VMEM((2, 2, piece, LANES), f32),
            pltpu.VMEM((2, piece, LANES), bf),
            pltpu.VMEM((2, chips, piece, LANES), bf),
            pltpu.VMEM((2, 2, piece, LANES), bf),
            pltpu.VMEM((2, owners * piece, LANES), bf),
            dma((4,)), dma((3,)),
            dma((2, n, owners)), dma((2, n, owners)),
            dma((2, n, chips)), dma((2, n, chips)),
            dma((2, n, owners)), dma((2, n, owners)),
        ],
        cost_estimate=pl.CostEstimate(
            flops=flops, bytes_accessed=14 * tok * width, transcendentals=2 * tok * width),
        compiler_params=pltpu.CompilerParams(
            collective_id=0, has_side_effects=True, vmem_limit_bytes=48 * 1024 * 1024),
    )(query_raw.T, key_raw.T, values.T, norm_gain, grad_out.T)
    return tuple(g.T for g in grads)


def solution(mesh):
    split = P(("frame", "row"), None)
    return jax.shard_map(
        functools.partial(body, mesh.shape["row"], mesh.shape["frame"]),
        mesh=mesh,
        in_specs=(split, split, split, P(), split),
        out_specs=(split, split, split),
        check_vma=False,
    )
```

```python
import functools

import jax
import jax.numpy as jnp
from jax import lax
from jax.experimental import pallas as pl
from jax.experimental.pallas import tpu as pltpu
from jax.sharding import PartitionSpec as P

HEAD_DIM = 112
LANES = 128
OWNERS = 4
GROUP = 4
MESH = pl.DeviceIdType.MESH
TN = (((0,), (0,)), ((), ()))
NT = (((1,), (1,)), ((), ()))
NN = (((1,), (0,)), ((), ()))


def dot(a, b, dims):
    return lax.dot_general(a, b, dims, preferred_element_type=jnp.float32)


def kernel(groups, pieces, rows_n, frames_n, q_hbm, k_hbm, v_hbm, gain_ref, g_hbm,
           gq_hbm, gk_hbm, gv_hbm,
           q_raw, k_raw, v_raw, g_raw, gq_out, gk_out, gv_out,
           q_feat, k_feat, gain, q_slope, k_slope, weighted, grad_att,
           send_buf, rs_buf, share, zh_send, zh_buf, fr_send, fr_buf, ag_send, whole,
           in_sem, out_sem, rs_ssem, rs_rsem, zh_ssem, zh_rsem, fr_ssem, fr_rsem, ag_ssem, ag_rsem):
    D = HEAD_DIM
    owners = OWNERS
    pairs = rows_n // 2
    chips = frames_n // 2
    frame, row = lax.axis_index("frame"), lax.axis_index("row")
    chip, core = frame // 2, frame % 2
    pair, half = row // 2, row % 2
    me = half * 2 + core

    def column_id(step):
        dest = lax.rem(me + step, owners)
        return (chip * 2 + dest % 2, pair * 2 + dest // 2)

    def pair_id(step):
        return (frame, lax.rem(pair + step, pairs) * 2 + half)

    def chip_id(step):
        return (lax.rem(chip + step, chips) * 2 + core, row)

    loads = [
        pltpu.make_async_copy(src, dst, in_sem.at[i])
        for i, (src, dst) in enumerate(
            [(k_hbm, k_raw), (v_hbm, v_raw), (q_hbm, q_raw), (g_hbm, g_raw)])
    ]
    for c in loads:
        c.start()

    barrier = pltpu.get_barrier_semaphore()
    for j in range(1, owners):
        pl.semaphore_signal(barrier, inc=1, device_id=column_id(j), device_id_type=MESH)
    for j in range(1, pairs):
        pl.semaphore_signal(barrier, inc=1, device_id=pair_id(j), device_id_type=MESH)
    for j in range(1, chips):
        pl.semaphore_signal(barrier, inc=1, device_id=chip_id(j), device_id_type=MESH)

    def cols(h):
        return slice(h * D, (h + 1) * D)

    base_of = [sum(pieces[:g]) * owners for g in range(len(groups))]
    slot_of = [sum(pieces[:g]) for g in range(len(groups))]

    def rows_of(g, index):
        return pl.ds(pl.multiple_of(base_of[g] + index * pieces[g], 16), pieces[g])

    def slot(g):
        return pl.ds(slot_of[g], pieces[g])

    def phi(raw):
        low = jnp.exp(jnp.minimum(raw, 0.0))
        return jnp.where(raw > 0, raw + 1.0, low), jnp.where(raw > 0, 1.0, low)

    def rs_copy(p, g, j):
        dest = lax.rem(me + j, owners)
        return pltpu.make_async_remote_copy(
            src_ref=send_buf.at[p, rows_of(g, dest)],
            dst_ref=rs_buf.at[p, j, slot(g)],
            send_sem=rs_ssem.at[p, g, j], recv_sem=rs_rsem.at[p, g, j],
            device_id=column_id(j), device_id_type=MESH)

    def both(g):
        return pl.ds(2 * slot_of[g], 2 * pieces[g])

    def zh_copy(p, g, j):
        return pltpu.make_async_remote_copy(
            src_ref=zh_send.at[p, both(g)], dst_ref=zh_buf.at[p, j, both(g)],
            send_sem=zh_ssem.at[p, g, j], recv_sem=zh_rsem.at[p, g, j],
            device_id=pair_id(j), device_id_type=MESH)

    def fr_copy(p, g, j):
        return pltpu.make_async_remote_copy(
            src_ref=fr_send.at[p, slot(g)], dst_ref=fr_buf.at[p, j, slot(g)],
            send_sem=fr_ssem.at[p, g, j], recv_sem=fr_rsem.at[p, g, j],
            device_id=chip_id(j), device_id_type=MESH)

    def ag_copy(p, g, j):
        return pltpu.make_async_remote_copy(
            src_ref=ag_send.at[p, j % 2, slot(g)],
            dst_ref=whole.at[p, rows_of(g, me)],
            send_sem=ag_ssem.at[p, g, j], recv_sem=ag_rsem.at[p, g, j],
            device_id=column_id(j), device_id_type=MESH)

    def ag_wait(p, g, j):
        src = lax.rem(me - j + owners, owners)
        pltpu.make_async_remote_copy(
            src_ref=ag_send.at[p, j % 2, slot(g)],
            dst_ref=whole.at[p, rows_of(g, src)],
            send_sem=ag_ssem.at[p, g, j], recv_sem=ag_rsem.at[p, g, j],
            device_id=column_id(j), device_id_type=MESH).wait_recv()

    def start_rs(p, g):
        for j in range(1, owners):
            rs_copy(p, g, j).start()

    def reduce_rows(p, g):
        mine = send_buf[p, rows_of(g, me), :].astype(jnp.float32)
        other = None
        for j in range(1, owners):
            rs_copy(p, g, j).wait_recv()
        for j in range(1, owners):
            block = rs_buf[p, j, slot(g), :].astype(jnp.float32)
            if j % 2 == 0:
                mine = mine + block
            else:
                other = block if other is None else other + block
        share[p, 0, slot(g), :] = mine
        share[p, 1, slot(g), :] = other
        zh_send[p, both(g), :] = jnp.concatenate([mine, other], axis=0).astype(jnp.bfloat16)
        for j in range(1, pairs):
            zh_copy(p, g, j).start()

    def reduce_pairs(p, g):
        for j in range(1, pairs):
            zh_copy(p, g, j).wait_recv()
        mine, other = share[p, 0, slot(g), :], share[p, 1, slot(g), :]
        for j in range(1, pairs):
            block = zh_buf[p, j, both(g), :].astype(jnp.float32)
            mine = mine + block[:pieces[g]]
            other = other + block[pieces[g]:]
        share[p, 0, slot(g), :] = mine
        share[p, 1, slot(g), :] = other
        fr_send[p, slot(g), :] = (mine + other).astype(jnp.bfloat16)
        for j in range(1, chips):
            fr_copy(p, g, j).start()

    def scan_frames(p, g):
        for j in range(1, chips):
            fr_copy(p, g, j).wait_recv()
        base = jnp.zeros((pieces[g], LANES), jnp.float32)
        for j in range(1, chips):
            keep = (j <= chip) if p == 0 else (j > chip)
            base = base + jnp.where(keep, fr_buf[p, j, slot(g), :].astype(jnp.float32), 0.0)
        mine, other = share[p, 0, slot(g), :], share[p, 1, slot(g), :]
        own_last = (core == 1) if p == 0 else (core == 0)
        ag_send[p, 0, slot(g), :] = (base + mine + jnp.where(own_last, other, 0.0)).astype(jnp.bfloat16)
        ag_send[p, 1, slot(g), :] = (base + other + jnp.where(own_last, 0.0, mine)).astype(jnp.bfloat16)
        for j in range(1, owners):
            ag_copy(p, g, j).start()
        whole[p, rows_of(g, me), :] = ag_send[p, 0, slot(g), :]

    def wait_whole(p, g):
        for j in range(1, owners):
            ag_wait(p, g, j)

    span = range(len(groups))

    def head_state(p, g, i):
        return whole[p, base_of[g] + i * D:base_of[g] + (i + 1) * D, :D]

    loads[0].wait()
    loads[1].wait()
    for g in span:
        for i, h in enumerate(groups[g]):
            feat, slope = phi(k_raw[cols(h), :].astype(jnp.float32))
            feat = feat.astype(jnp.bfloat16)
            val = v_raw[cols(h), :]
            k_feat[h] = feat
            k_slope[h] = slope
            send_buf[0, base_of[g] + i * D:base_of[g] + (i + 1) * D, :D] = dot(feat, val, NT).astype(jnp.bfloat16)
        if g == 0:
            pl.semaphore_wait(barrier, owners - 1 + pairs - 1 + chips - 1)
        start_rs(0, g)

    loads[2].wait()
    loads[3].wait()
    tok, width = q_raw.shape[1], q_raw.shape[0]
    gain[...] = jnp.broadcast_to(gain_ref[...].reshape(1, width), (tok, width)).T
    for g in span:
        for h in groups[g]:
            feat, slope = phi(q_raw[cols(h), :].astype(jnp.float32))
            q_feat[h] = feat.astype(jnp.bfloat16)
            q_slope[h] = slope
            weighted[h] = g_raw[cols(h), :].astype(jnp.float32) * gain[cols(h), :]

    def query_side(g):
        wait_whole(0, g)
        for i, h in enumerate(groups[g]):
            att = dot(head_state(0, g, i), q_feat[h], TN)
            w = weighted[h]
            inv = lax.rsqrt(jnp.mean(att * att, axis=0, keepdims=True) + 1e-6)
            inner = jnp.mean(w * att, axis=0, keepdims=True)
            ga = (inv * w - att * (inv * inv * inv * inner)).astype(jnp.bfloat16)
            grad_att[h] = ga
            row0 = base_of[g] + i * D
            send_buf[1, row0:row0 + D, :D] = dot(q_feat[h], ga, NT).astype(jnp.bfloat16)
        start_rs(1, g)

    def grad_query(g):
        for i, h in enumerate(groups[g]):
            gq = dot(head_state(0, g, i), grad_att[h], NN) * q_slope[h]
            gq_out[cols(h), :] = gq.astype(jnp.bfloat16)

    def key_side(g):
        wait_whole(1, g)
        for i, h in enumerate(groups[g]):
            adj = head_state(1, g, i)
            gv_out[cols(h), :] = dot(adj, k_feat[h], TN).astype(jnp.bfloat16)
            gk_out[cols(h), :] = (dot(adj, v_raw[cols(h), :], NN) * k_slope[h]).astype(jnp.bfloat16)

    def skewed(p, last, beside):
        stages = [reduce_rows, reduce_pairs, scan_frames]
        for t in range(len(groups) + len(stages)):
            for at, stage in enumerate(stages):
                if 0 <= t - at < len(groups):
                    stage(p, t - at)
            if beside is not None and t < len(groups):
                beside(t)
            if 0 <= t - len(stages) < len(groups):
                last(t - len(stages))

    stores = [
        pltpu.make_async_copy(src, dst, out_sem.at[i])
        for i, (src, dst) in enumerate([(gq_out, gq_hbm), (gk_out, gk_hbm), (gv_out, gv_hbm)])
    ]
    skewed(0, query_side, None)
    skewed(1, key_side, grad_query)
    stores[0].start()
    stores[1].start()
    stores[2].start()

    for p in range(2):
        for g in span:
            for j in range(1, owners):
                rs_copy(p, g, j).wait_send()
                ag_copy(p, g, j).wait_send()
            for j in range(1, pairs):
                zh_copy(p, g, j).wait_send()
            for j in range(1, chips):
                fr_copy(p, g, j).wait_send()
    for c in stores:
        c.wait()


def body(rows_n, frames_n, query_raw, key_raw, values, norm_gain, grad_out):
    tok, width = query_raw.shape
    heads = width // HEAD_DIM
    owners, pairs, chips = OWNERS, rows_n // 2, frames_n // 2
    groups = [list(range(s, min(s + GROUP, heads))) for s in range(0, heads, GROUP)]
    n = len(groups)
    unit = 16 * owners
    pieces = [-(-len(g) * HEAD_DIM // unit) * 16 for g in groups]
    piece = sum(pieces)
    bf, f32 = jnp.bfloat16, jnp.float32
    raw = pltpu.VMEM((width, tok), bf)
    per_head = lambda t: pltpu.VMEM((heads, HEAD_DIM, tok), t)
    dma = pltpu.SemaphoreType.DMA
    out = jax.ShapeDtypeStruct((width, tok), bf)
    flops = 12 * tok * heads * HEAD_DIM * HEAD_DIM
    hbm = pl.BlockSpec(memory_space=pl.ANY)
    grads = pl.pallas_call(
        functools.partial(kernel, groups, pieces, rows_n, frames_n),
        out_shape=(out, out, out),
        in_specs=[hbm, hbm, hbm, pl.BlockSpec(memory_space=pltpu.VMEM), hbm],
        out_specs=(hbm, hbm, hbm),
        scratch_shapes=[
            raw, raw, raw, raw, raw, raw, raw,
            per_head(bf), per_head(bf), pltpu.VMEM((width, tok), f32),
            per_head(f32), per_head(f32), per_head(f32), per_head(bf),
            pltpu.VMEM((2, owners * piece, LANES), bf),
            pltpu.VMEM((2, owners, piece, LANES), bf),
            pltpu.VMEM((2, 2, piece, LANES), f32),
            pltpu.VMEM((2, 2 * piece, LANES), bf),
            pltpu.VMEM((2, pairs, 2 * piece, LANES), bf),
            pltpu.VMEM((2, piece, LANES), bf),
            pltpu.VMEM((2, chips, piece, LANES), bf),
            pltpu.VMEM((2, 2, piece, LANES), bf),
            pltpu.VMEM((2, owners * piece, LANES), bf),
            dma((4,)), dma((3,)),
            dma((2, n, owners)), dma((2, n, owners)),
            dma((2, n, pairs)), dma((2, n, pairs)),
            dma((2, n, chips)), dma((2, n, chips)),
            dma((2, n, owners)), dma((2, n, owners)),
        ],
        cost_estimate=pl.CostEstimate(
            flops=flops, bytes_accessed=14 * tok * width, transcendentals=2 * tok * width),
        compiler_params=pltpu.CompilerParams(
            collective_id=0, has_side_effects=True, vmem_limit_bytes=60 * 1024 * 1024),
    )(query_raw.T, key_raw.T, values.T, norm_gain, grad_out.T)
    return tuple(g.T for g in grads)


def solution(mesh):
    split = P(("frame", "row"), None)
    return jax.shard_map(
        functools.partial(body, mesh.shape["row"], mesh.shape["frame"]),
        mesh=mesh,
        in_specs=(split, split, split, P(), split),
        out_specs=(split, split, split),
        check_vma=False,
    )
```

```python
import functools

import jax
import jax.numpy as jnp
from jax import lax
from jax.experimental import pallas as pl
from jax.experimental.pallas import tpu as pltpu
from jax.sharding import PartitionSpec as P

HEAD_DIM = 112
LANES = 128
OWNERS = 4
GROUP = 4
MESH = pl.DeviceIdType.MESH
TN = (((0,), (0,)), ((), ()))
NT = (((1,), (1,)), ((), ()))
NN = (((1,), (0,)), ((), ()))


def dot(a, b, dims):
    return lax.dot_general(a, b, dims, preferred_element_type=jnp.float32)


def kernel(groups, pieces, rows_n, frames_n, q_hbm, k_hbm, v_hbm, gain_ref, g_hbm,
           gq_hbm, gk_hbm, gv_hbm,
           q_raw, k_raw, v_raw, g_raw, gq_out, gk_out, gv_out,
           q_feat, k_feat, gain, q_slope, k_slope, weighted, grad_att,
           send_buf, rs_buf, share, zh_send, zh_buf, fr_send, fr_buf, ag_send, whole,
           in_sem, out_sem, rs_ssem, rs_rsem, zh_ssem, zh_rsem, fr_ssem, fr_rsem, ag_ssem, ag_rsem):
    D = HEAD_DIM
    owners = OWNERS
    pairs = rows_n // 2
    chips = frames_n // 2
    frame, row = lax.axis_index("frame"), lax.axis_index("row")
    chip, core = frame // 2, frame % 2
    pair, half = row // 2, row % 2
    me = half * 2 + core

    def column_id(step):
        dest = lax.rem(me + step, owners)
        return (chip * 2 + dest % 2, pair * 2 + dest // 2)

    def pair_id(step):
        return (frame, lax.rem(pair + step, pairs) * 2 + half)

    def chip_id(step):
        return (lax.rem(chip + step, chips) * 2 + core, row)

    loads = [
        pltpu.make_async_copy(src, dst, in_sem.at[i])
        for i, (src, dst) in enumerate(
            [(k_hbm, k_raw), (v_hbm, v_raw), (q_hbm, q_raw), (g_hbm, g_raw)])
    ]
    for c in loads:
        c.start()

    barrier = pltpu.get_barrier_semaphore()
    for j in range(1, owners):
        pl.semaphore_signal(barrier, inc=1, device_id=column_id(j), device_id_type=MESH)
    for j in range(1, pairs):
        pl.semaphore_signal(barrier, inc=1, device_id=pair_id(j), device_id_type=MESH)
    for j in range(1, chips):
        pl.semaphore_signal(barrier, inc=1, device_id=chip_id(j), device_id_type=MESH)

    def cols(h):
        return slice(h * D, (h + 1) * D)

    base_of = [sum(pieces[:g]) * owners for g in range(len(groups))]
    slot_of = [sum(pieces[:g]) for g in range(len(groups))]

    def rows_of(g, index):
        return pl.ds(pl.multiple_of(base_of[g] + index * pieces[g], 16), pieces[g])

    def slot(g):
        return pl.ds(slot_of[g], pieces[g])

    def phi(raw):
        low = jnp.exp(jnp.minimum(raw, 0.0))
        return jnp.where(raw > 0, raw + 1.0, low), jnp.where(raw > 0, 1.0, low)

    def rs_copy(p, g, j):
        dest = lax.rem(me + j, owners)
        return pltpu.make_async_remote_copy(
            src_ref=send_buf.at[p, rows_of(g, dest)],
            dst_ref=rs_buf.at[p, j, slot(g)],
            send_sem=rs_ssem.at[p, g, j], recv_sem=rs_rsem.at[p, g, j],
            device_id=column_id(j), device_id_type=MESH)

    def both(g):
        return pl.ds(2 * slot_of[g], 2 * pieces[g])

    def zh_copy(p, g, j):
        return pltpu.make_async_remote_copy(
            src_ref=zh_send.at[p, both(g)], dst_ref=zh_buf.at[p, j, both(g)],
            send_sem=zh_ssem.at[p, g, j], recv_sem=zh_rsem.at[p, g, j],
            device_id=pair_id(j), device_id_type=MESH)

    def fr_copy(p, g, j):
        return pltpu.make_async_remote_copy(
            src_ref=fr_send.at[p, slot(g)], dst_ref=fr_buf.at[p, j, slot(g)],
            send_sem=fr_ssem.at[p, g, j], recv_sem=fr_rsem.at[p, g, j],
            device_id=chip_id(j), device_id_type=MESH)

    def ag_copy(p, g, j):
        return pltpu.make_async_remote_copy(
            src_ref=ag_send.at[p, j % 2, slot(g)],
            dst_ref=whole.at[p, rows_of(g, me)],
            send_sem=ag_ssem.at[p, g, j], recv_sem=ag_rsem.at[p, g, j],
            device_id=column_id(j), device_id_type=MESH)

    def ag_wait(p, g, j):
        src = lax.rem(me - j + owners, owners)
        pltpu.make_async_remote_copy(
            src_ref=ag_send.at[p, j % 2, slot(g)],
            dst_ref=whole.at[p, rows_of(g, src)],
            send_sem=ag_ssem.at[p, g, j], recv_sem=ag_rsem.at[p, g, j],
            device_id=column_id(j), device_id_type=MESH).wait_recv()

    def start_rs(p, g):
        for j in range(1, owners):
            rs_copy(p, g, j).start()

    def reduce_rows(p, g):
        mine = send_buf[p, rows_of(g, me), :].astype(jnp.float32)
        other = None
        for j in range(1, owners):
            rs_copy(p, g, j).wait_recv()
        for j in range(1, owners):
            block = rs_buf[p, j, slot(g), :].astype(jnp.float32)
            if j % 2 == 0:
                mine = mine + block
            else:
                other = block if other is None else other + block
        share[p, 0, slot(g), :] = mine
        share[p, 1, slot(g), :] = other
        zh_send[p, both(g), :] = jnp.concatenate([mine, other], axis=0).astype(jnp.bfloat16)
        for j in range(1, pairs):
            zh_copy(p, g, j).start()

    def reduce_pairs(p, g):
        for j in range(1, pairs):
            zh_copy(p, g, j).wait_recv()
        mine, other = share[p, 0, slot(g), :], share[p, 1, slot(g), :]
        for j in range(1, pairs):
            block = zh_buf[p, j, both(g), :].astype(jnp.float32)
            mine = mine + block[:pieces[g]]
            other = other + block[pieces[g]:]
        share[p, 0, slot(g), :] = mine
        share[p, 1, slot(g), :] = other
        fr_send[p, slot(g), :] = (mine + other).astype(jnp.bfloat16)
        for j in range(1, chips):
            fr_copy(p, g, j).start()

    def scan_frames(p, g):
        for j in range(1, chips):
            fr_copy(p, g, j).wait_recv()
        base = jnp.zeros((pieces[g], LANES), jnp.float32)
        for j in range(1, chips):
            keep = (j <= chip) if p == 0 else (j > chip)
            base = base + jnp.where(keep, fr_buf[p, j, slot(g), :].astype(jnp.float32), 0.0)
        mine, other = share[p, 0, slot(g), :], share[p, 1, slot(g), :]
        own_last = (core == 1) if p == 0 else (core == 0)
        ag_send[p, 0, slot(g), :] = (base + mine + jnp.where(own_last, other, 0.0)).astype(jnp.bfloat16)
        ag_send[p, 1, slot(g), :] = (base + other + jnp.where(own_last, 0.0, mine)).astype(jnp.bfloat16)
        for j in range(1, owners):
            ag_copy(p, g, j).start()
        whole[p, rows_of(g, me), :] = ag_send[p, 0, slot(g), :]

    def wait_whole(p, g):
        for j in range(1, owners):
            ag_wait(p, g, j)

    span = range(len(groups))

    def head_state(p, g, i):
        return whole[p, base_of[g] + i * D:base_of[g] + (i + 1) * D, :D]

    loads[0].wait()
    loads[1].wait()
    for g in span:
        for i, h in enumerate(groups[g]):
            feat, slope = phi(k_raw[cols(h), :].astype(jnp.float32))
            feat = feat.astype(jnp.bfloat16)
            val = v_raw[cols(h), :]
            k_feat[h] = feat
            k_slope[h] = slope
            send_buf[0, base_of[g] + i * D:base_of[g] + (i + 1) * D, :D] = dot(feat, val, NT).astype(jnp.bfloat16)
        if g == 0:
            pl.semaphore_wait(barrier, owners - 1 + pairs - 1 + chips - 1)
        start_rs(0, g)

    loads[2].wait()
    loads[3].wait()
    tok, width = q_raw.shape[1], q_raw.shape[0]
    gain[...] = jnp.broadcast_to(gain_ref[...].reshape(1, width), (tok, width)).T
    for g in span:
        for h in groups[g]:
            feat, slope = phi(q_raw[cols(h), :].astype(jnp.float32))
            q_feat[h] = feat.astype(jnp.bfloat16)
            q_slope[h] = slope
            weighted[h] = g_raw[cols(h), :].astype(jnp.float32) * gain[cols(h), :]

    def query_side(g):
        wait_whole(0, g)
        for i, h in enumerate(groups[g]):
            att = dot(head_state(0, g, i), q_feat[h], TN)
            w = weighted[h]
            inv = lax.rsqrt(jnp.mean(att * att, axis=0, keepdims=True) + 1e-6)
            inner = jnp.mean(w * att, axis=0, keepdims=True)
            ga = (inv * w - att * (inv * inv * inv * inner)).astype(jnp.bfloat16)
            grad_att[h] = ga
            row0 = base_of[g] + i * D
            send_buf[1, row0:row0 + D, :D] = dot(q_feat[h], ga, NT).astype(jnp.bfloat16)
        start_rs(1, g)

    def grad_query(g):
        for i, h in enumerate(groups[g]):
            gq = dot(head_state(0, g, i), grad_att[h], NN) * q_slope[h]
            gq_out[cols(h), :] = gq.astype(jnp.bfloat16)

    def key_side(g):
        wait_whole(1, g)
        for i, h in enumerate(groups[g]):
            adj = head_state(1, g, i)
            gv_out[cols(h), :] = dot(adj, k_feat[h], TN).astype(jnp.bfloat16)
            gk_out[cols(h), :] = (dot(adj, v_raw[cols(h), :], NN) * k_slope[h]).astype(jnp.bfloat16)

    def staged(p, last, beside):
        for stage in (reduce_rows, reduce_pairs, scan_frames):
            for g in span:
                stage(p, g)
            if beside is not None and stage is not scan_frames:
                for g in span:
                    if (g == 0) == (stage is reduce_rows):
                        beside(g)
        for g in span:
            last(g)

    stores = [
        pltpu.make_async_copy(src, dst, out_sem.at[i])
        for i, (src, dst) in enumerate([(gq_out, gq_hbm), (gk_out, gk_hbm), (gv_out, gv_hbm)])
    ]
    staged(0, query_side, None)
    staged(1, key_side, grad_query)
    stores[0].start()
    stores[1].start()
    stores[2].start()

    for p in range(2):
        for g in span:
            for j in range(1, owners):
                rs_copy(p, g, j).wait_send()
                ag_copy(p, g, j).wait_send()
            for j in range(1, pairs):
                zh_copy(p, g, j).wait_send()
            for j in range(1, chips):
                fr_copy(p, g, j).wait_send()
    for c in stores:
        c.wait()


def body(rows_n, frames_n, query_raw, key_raw, values, norm_gain, grad_out):
    tok, width = query_raw.shape
    heads = width // HEAD_DIM
    owners, pairs, chips = OWNERS, rows_n // 2, frames_n // 2
    groups = [list(range(s, min(s + GROUP, heads))) for s in range(0, heads, GROUP)]
    n = len(groups)
    unit = 16 * owners
    pieces = [-(-len(g) * HEAD_DIM // unit) * 16 for g in groups]
    piece = sum(pieces)
    bf, f32 = jnp.bfloat16, jnp.float32
    raw = pltpu.VMEM((width, tok), bf)
    per_head = lambda t: pltpu.VMEM((heads, HEAD_DIM, tok), t)
    dma = pltpu.SemaphoreType.DMA
    out = jax.ShapeDtypeStruct((width, tok), bf)
    flops = 12 * tok * heads * HEAD_DIM * HEAD_DIM
    hbm = pl.BlockSpec(memory_space=pl.ANY)
    grads = pl.pallas_call(
        functools.partial(kernel, groups, pieces, rows_n, frames_n),
        out_shape=(out, out, out),
        in_specs=[hbm, hbm, hbm, pl.BlockSpec(memory_space=pltpu.VMEM), hbm],
        out_specs=(hbm, hbm, hbm),
        scratch_shapes=[
            raw, raw, raw, raw, raw, raw, raw,
            per_head(bf), per_head(bf), pltpu.VMEM((width, tok), f32),
            per_head(f32), per_head(f32), per_head(f32), per_head(bf),
            pltpu.VMEM((2, owners * piece, LANES), bf),
            pltpu.VMEM((2, owners, piece, LANES), bf),
            pltpu.VMEM((2, 2, piece, LANES), f32),
            pltpu.VMEM((2, 2 * piece, LANES), bf),
            pltpu.VMEM((2, pairs, 2 * piece, LANES), bf),
            pltpu.VMEM((2, piece, LANES), bf),
            pltpu.VMEM((2, chips, piece, LANES), bf),
            pltpu.VMEM((2, 2, piece, LANES), bf),
            pltpu.VMEM((2, owners * piece, LANES), bf),
            dma((4,)), dma((3,)),
            dma((2, n, owners)), dma((2, n, owners)),
            dma((2, n, pairs)), dma((2, n, pairs)),
            dma((2, n, chips)), dma((2, n, chips)),
            dma((2, n, owners)), dma((2, n, owners)),
        ],
        cost_estimate=pl.CostEstimate(
            flops=flops, bytes_accessed=14 * tok * width, transcendentals=2 * tok * width),
        compiler_params=pltpu.CompilerParams(
            collective_id=0, has_side_effects=True, vmem_limit_bytes=60 * 1024 * 1024),
    )(query_raw.T, key_raw.T, values.T, norm_gain, grad_out.T)
    return tuple(g.T for g in grads)


def solution(mesh):
    split = P(("frame", "row"), None)
    return jax.shard_map(
        functools.partial(body, mesh.shape["row"], mesh.shape["frame"]),
        mesh=mesh,
        in_specs=(split, split, split, P(), split),
        out_specs=(split, split, split),
        check_vma=False,
    )
```

```python
import functools

import jax
import jax.numpy as jnp
from jax import lax
from jax.experimental import pallas as pl
from jax.experimental.pallas import tpu as pltpu
from jax.sharding import PartitionSpec as P

HEAD_DIM = 112
LANES = 128
OWNERS = 4
GROUP = 5
MESH = pl.DeviceIdType.MESH
TN = (((0,), (0,)), ((), ()))
NT = (((1,), (1,)), ((), ()))
NN = (((1,), (0,)), ((), ()))


def dot(a, b, dims):
    return lax.dot_general(a, b, dims, preferred_element_type=jnp.float32)


def kernel(groups, pieces, rows_n, frames_n, q_hbm, k_hbm, v_hbm, gain_ref, g_hbm,
           gq_hbm, gk_hbm, gv_hbm,
           q_raw, k_raw, v_raw, g_raw, gq_out, gk_out, gv_out,
           q_feat, k_feat, gain, q_slope, k_slope, weighted, grad_att,
           send_buf, rs_buf, share, zh_send, zh_buf, fr_send, fr_buf, ag_send, whole,
           in_sem, out_sem, rs_ssem, rs_rsem, zh_ssem, zh_rsem, fr_ssem, fr_rsem, ag_ssem, ag_rsem):
    D = HEAD_DIM
    owners = OWNERS
    pairs = rows_n // 2
    chips = frames_n // 2
    frame, row = lax.axis_index("frame"), lax.axis_index("row")
    chip, core = frame // 2, frame % 2
    pair, half = row // 2, row % 2
    me = half * 2 + core

    def column_id(step):
        dest = lax.rem(me + step, owners)
        return (chip * 2 + dest % 2, pair * 2 + dest // 2)

    def pair_id(step):
        return (frame, lax.rem(pair + step, pairs) * 2 + half)

    def chip_id(step):
        return (lax.rem(chip + step, chips) * 2 + core, row)

    loads = [
        pltpu.make_async_copy(src, dst, in_sem.at[i])
        for i, (src, dst) in enumerate(
            [(k_hbm, k_raw), (v_hbm, v_raw), (q_hbm, q_raw), (g_hbm, g_raw)])
    ]
    for c in loads:
        c.start()

    barrier = pltpu.get_barrier_semaphore()
    for j in range(1, owners):
        pl.semaphore_signal(barrier, inc=1, device_id=column_id(j), device_id_type=MESH)
    for j in range(1, pairs):
        pl.semaphore_signal(barrier, inc=1, device_id=pair_id(j), device_id_type=MESH)
    for j in range(1, chips):
        pl.semaphore_signal(barrier, inc=1, device_id=chip_id(j), device_id_type=MESH)

    def cols(h):
        return slice(h * D, (h + 1) * D)

    base_of = [sum(pieces[:g]) * owners for g in range(len(groups))]
    slot_of = [sum(pieces[:g]) for g in range(len(groups))]

    def rows_of(g, index):
        return pl.ds(pl.multiple_of(base_of[g] + index * pieces[g], 16), pieces[g])

    def slot(g):
        return pl.ds(slot_of[g], pieces[g])

    def phi(raw):
        low = jnp.exp(jnp.minimum(raw, 0.0))
        return jnp.where(raw > 0, raw + 1.0, low), jnp.where(raw > 0, 1.0, low)

    def rs_copy(p, g, j):
        dest = lax.rem(me + j, owners)
        return pltpu.make_async_remote_copy(
            src_ref=send_buf.at[p, rows_of(g, dest)],
            dst_ref=rs_buf.at[p, j, slot(g)],
            send_sem=rs_ssem.at[p, g, j], recv_sem=rs_rsem.at[p, g, j],
            device_id=column_id(j), device_id_type=MESH)

    def both(g):
        return pl.ds(2 * slot_of[g], 2 * pieces[g])

    def zh_copy(p, g, j):
        return pltpu.make_async_remote_copy(
            src_ref=zh_send.at[p, both(g)], dst_ref=zh_buf.at[p, j, both(g)],
            send_sem=zh_ssem.at[p, g, j], recv_sem=zh_rsem.at[p, g, j],
            device_id=pair_id(j), device_id_type=MESH)

    def fr_copy(p, g, j):
        return pltpu.make_async_remote_copy(
            src_ref=fr_send.at[p, slot(g)], dst_ref=fr_buf.at[p, j, slot(g)],
            send_sem=fr_ssem.at[p, g, j], recv_sem=fr_rsem.at[p, g, j],
            device_id=chip_id(j), device_id_type=MESH)

    def ag_copy(p, g, j):
        return pltpu.make_async_remote_copy(
            src_ref=ag_send.at[p, j % 2, slot(g)],
            dst_ref=whole.at[p, rows_of(g, me)],
            send_sem=ag_ssem.at[p, g, j], recv_sem=ag_rsem.at[p, g, j],
            device_id=column_id(j), device_id_type=MESH)

    def ag_wait(p, g, j):
        src = lax.rem(me - j + owners, owners)
        pltpu.make_async_remote_copy(
            src_ref=ag_send.at[p, j % 2, slot(g)],
            dst_ref=whole.at[p, rows_of(g, src)],
            send_sem=ag_ssem.at[p, g, j], recv_sem=ag_rsem.at[p, g, j],
            device_id=column_id(j), device_id_type=MESH).wait_recv()

    def start_rs(p, g):
        for j in range(1, owners):
            rs_copy(p, g, j).start()

    def reduce_rows(p, g):
        mine = send_buf[p, rows_of(g, me), :].astype(jnp.float32)
        other = None
        for j in range(1, owners):
            rs_copy(p, g, j).wait_recv()
        for j in range(1, owners):
            block = rs_buf[p, j, slot(g), :].astype(jnp.float32)
            if j % 2 == 0:
                mine = mine + block
            else:
                other = block if other is None else other + block
        share[p, 0, slot(g), :] = mine
        share[p, 1, slot(g), :] = other
        zh_send[p, both(g), :] = jnp.concatenate([mine, other], axis=0).astype(jnp.bfloat16)
        for j in range(1, pairs):
            zh_copy(p, g, j).start()

    def reduce_pairs(p, g):
        for j in range(1, pairs):
            zh_copy(p, g, j).wait_recv()
        mine, other = share[p, 0, slot(g), :], share[p, 1, slot(g), :]
        for j in range(1, pairs):
            block = zh_buf[p, j, both(g), :].astype(jnp.float32)
            mine = mine + block[:pieces[g]]
            other = other + block[pieces[g]:]
        share[p, 0, slot(g), :] = mine
        share[p, 1, slot(g), :] = other
        fr_send[p, slot(g), :] = (mine + other).astype(jnp.bfloat16)
        for j in range(1, chips):
            fr_copy(p, g, j).start()

    def scan_frames(p, g):
        for j in range(1, chips):
            fr_copy(p, g, j).wait_recv()
        base = jnp.zeros((pieces[g], LANES), jnp.float32)
        for j in range(1, chips):
            keep = (j <= chip) if p == 0 else (j > chip)
            base = base + jnp.where(keep, fr_buf[p, j, slot(g), :].astype(jnp.float32), 0.0)
        mine, other = share[p, 0, slot(g), :], share[p, 1, slot(g), :]
        own_last = (core == 1) if p == 0 else (core == 0)
        ag_send[p, 0, slot(g), :] = (base + mine + jnp.where(own_last, other, 0.0)).astype(jnp.bfloat16)
        ag_send[p, 1, slot(g), :] = (base + other + jnp.where(own_last, 0.0, mine)).astype(jnp.bfloat16)
        for j in range(1, owners):
            ag_copy(p, g, j).start()
        whole[p, rows_of(g, me), :] = ag_send[p, 0, slot(g), :]

    def wait_whole(p, g):
        for j in range(1, owners):
            ag_wait(p, g, j)

    span = range(len(groups))

    def head_state(p, g, i):
        return whole[p, base_of[g] + i * D:base_of[g] + (i + 1) * D, :D]

    loads[0].wait()
    loads[1].wait()
    for g in span:
        for i, h in enumerate(groups[g]):
            feat, slope = phi(k_raw[cols(h), :].astype(jnp.float32))
            feat = feat.astype(jnp.bfloat16)
            val = v_raw[cols(h), :]
            k_feat[h] = feat
            k_slope[h] = slope
            send_buf[0, base_of[g] + i * D:base_of[g] + (i + 1) * D, :D] = dot(feat, val, NT).astype(jnp.bfloat16)
        if g == 0:
            pl.semaphore_wait(barrier, owners - 1 + pairs - 1 + chips - 1)
        start_rs(0, g)

    loads[2].wait()
    loads[3].wait()
    tok, width = q_raw.shape[1], q_raw.shape[0]
    gain[...] = jnp.broadcast_to(gain_ref[...].reshape(1, width), (tok, width)).T
    for g in span:
        for h in groups[g]:
            feat, slope = phi(q_raw[cols(h), :].astype(jnp.float32))
            q_feat[h] = feat.astype(jnp.bfloat16)
            q_slope[h] = slope
            weighted[h] = g_raw[cols(h), :].astype(jnp.float32) * gain[cols(h), :]

    def query_side(g):
        wait_whole(0, g)
        for i, h in enumerate(groups[g]):
            att = dot(head_state(0, g, i), q_feat[h], TN)
            w = weighted[h]
            inv = lax.rsqrt(jnp.mean(att * att, axis=0, keepdims=True) + 1e-6)
            inner = jnp.mean(w * att, axis=0, keepdims=True)
            ga = (inv * w - att * (inv * inv * inv * inner)).astype(jnp.bfloat16)
            grad_att[h] = ga
            row0 = base_of[g] + i * D
            send_buf[1, row0:row0 + D, :D] = dot(q_feat[h], ga, NT).astype(jnp.bfloat16)
        start_rs(1, g)

    def grad_query(g):
        for i, h in enumerate(groups[g]):
            gq = dot(head_state(0, g, i), grad_att[h], NN) * q_slope[h]
            gq_out[cols(h), :] = gq.astype(jnp.bfloat16)

    def key_side(g):
        wait_whole(1, g)
        for i, h in enumerate(groups[g]):
            adj = head_state(1, g, i)
            gv_out[cols(h), :] = dot(adj, k_feat[h], TN).astype(jnp.bfloat16)
            gk_out[cols(h), :] = (dot(adj, v_raw[cols(h), :], NN) * k_slope[h]).astype(jnp.bfloat16)

    def staged(p, last, beside):
        for stage in (reduce_rows, reduce_pairs, scan_frames):
            for g in span:
                stage(p, g)
            if beside is not None and stage is not scan_frames:
                for g in span:
                    if (g == 0) == (stage is reduce_rows):
                        beside(g)
        for g in span:
            last(g)

    stores = [
        pltpu.make_async_copy(src, dst, out_sem.at[i])
        for i, (src, dst) in enumerate([(gq_out, gq_hbm), (gk_out, gk_hbm), (gv_out, gv_hbm)])
    ]
    staged(0, query_side, None)
    staged(1, key_side, grad_query)
    stores[0].start()
    stores[1].start()
    stores[2].start()

    for p in range(2):
        for g in span:
            for j in range(1, owners):
                rs_copy(p, g, j).wait_send()
                ag_copy(p, g, j).wait_send()
            for j in range(1, pairs):
                zh_copy(p, g, j).wait_send()
            for j in range(1, chips):
                fr_copy(p, g, j).wait_send()
    for c in stores:
        c.wait()


def body(rows_n, frames_n, query_raw, key_raw, values, norm_gain, grad_out):
    tok, width = query_raw.shape
    heads = width // HEAD_DIM
    owners, pairs, chips = OWNERS, rows_n // 2, frames_n // 2
    groups = [list(range(s, min(s + GROUP, heads))) for s in range(0, heads, GROUP)]
    n = len(groups)
    unit = 16 * owners
    pieces = [-(-len(g) * HEAD_DIM // unit) * 16 for g in groups]
    piece = sum(pieces)
    bf, f32 = jnp.bfloat16, jnp.float32
    raw = pltpu.VMEM((width, tok), bf)
    per_head = lambda t: pltpu.VMEM((heads, HEAD_DIM, tok), t)
    dma = pltpu.SemaphoreType.DMA
    out = jax.ShapeDtypeStruct((width, tok), bf)
    flops = 12 * tok * heads * HEAD_DIM * HEAD_DIM
    hbm = pl.BlockSpec(memory_space=pl.ANY)
    grads = pl.pallas_call(
        functools.partial(kernel, groups, pieces, rows_n, frames_n),
        out_shape=(out, out, out),
        in_specs=[hbm, hbm, hbm, pl.BlockSpec(memory_space=pltpu.VMEM), hbm],
        out_specs=(hbm, hbm, hbm),
        scratch_shapes=[
            raw, raw, raw, raw, raw, raw, raw,
            per_head(bf), per_head(bf), pltpu.VMEM((width, tok), f32),
            per_head(f32), per_head(f32), per_head(f32), per_head(bf),
            pltpu.VMEM((2, owners * piece, LANES), bf),
            pltpu.VMEM((2, owners, piece, LANES), bf),
            pltpu.VMEM((2, 2, piece, LANES), f32),
            pltpu.VMEM((2, 2 * piece, LANES), bf),
            pltpu.VMEM((2, pairs, 2 * piece, LANES), bf),
            pltpu.VMEM((2, piece, LANES), bf),
            pltpu.VMEM((2, chips, piece, LANES), bf),
            pltpu.VMEM((2, 2, piece, LANES), bf),
            pltpu.VMEM((2, owners * piece, LANES), bf),
            dma((4,)), dma((3,)),
            dma((2, n, owners)), dma((2, n, owners)),
            dma((2, n, pairs)), dma((2, n, pairs)),
            dma((2, n, chips)), dma((2, n, chips)),
            dma((2, n, owners)), dma((2, n, owners)),
        ],
        cost_estimate=pl.CostEstimate(
            flops=flops, bytes_accessed=14 * tok * width, transcendentals=2 * tok * width),
        compiler_params=pltpu.CompilerParams(
            collective_id=0, has_side_effects=True, vmem_limit_bytes=60 * 1024 * 1024),
    )(query_raw.T, key_raw.T, values.T, norm_gain, grad_out.T)
    return tuple(g.T for g in grads)


def solution(mesh):
    split = P(("frame", "row"), None)
    return jax.shard_map(
        functools.partial(body, mesh.shape["row"], mesh.shape["frame"]),
        mesh=mesh,
        in_specs=(split, split, split, P(), split),
        out_specs=(split, split, split),
        check_vma=False,
    )
```

```python
import functools

import jax
import jax.numpy as jnp
from jax import lax
from jax.experimental import pallas as pl
from jax.experimental.pallas import tpu as pltpu
from jax.sharding import PartitionSpec as P

HEAD_DIM = 112
LANES = 128
OWNERS = 4
GROUP = 4
MESH = pl.DeviceIdType.MESH
TN = (((0,), (0,)), ((), ()))
NT = (((1,), (1,)), ((), ()))
NN = (((1,), (0,)), ((), ()))


def dot(a, b, dims):
    return lax.dot_general(a, b, dims, preferred_element_type=jnp.float32)


def kernel(groups, pieces, rows_n, frames_n, q_hbm, k_hbm, v_hbm, gain_ref, g_hbm,
           gq_hbm, gk_hbm, gv_hbm,
           q_raw, k_raw, v_raw, g_raw, gq_out, gk_out, gv_out,
           q_feat, k_feat, gain, q_slope, k_slope, weighted, grad_att,
           send_buf, rs_buf, share, zh_send, zh_buf, fr_send, fr_buf, ag_send, whole,
           in_sem, out_sem, rs_ssem, rs_rsem, zh_ssem, zh_rsem, fr_ssem, fr_rsem, ag_ssem, ag_rsem):
    D = HEAD_DIM
    owners = OWNERS
    pairs = rows_n // 2
    chips = frames_n // 2
    frame, row = lax.axis_index("frame"), lax.axis_index("row")
    chip, core = frame // 2, frame % 2
    pair, half = row // 2, row % 2
    me = half * 2 + core

    def column_id(step):
        dest = lax.rem(me + step, owners)
        return (chip * 2 + dest % 2, pair * 2 + dest // 2)

    def pair_id(step):
        return (frame, lax.rem(pair + step, pairs) * 2 + half)

    def chip_id(step):
        return (lax.rem(chip + step, chips) * 2 + core, row)

    loads = [
        pltpu.make_async_copy(src, dst, in_sem.at[i])
        for i, (src, dst) in enumerate(
            [(k_hbm, k_raw), (v_hbm, v_raw), (q_hbm, q_raw), (g_hbm, g_raw)])
    ]
    for c in loads:
        c.start()

    barrier = pltpu.get_barrier_semaphore()
    for j in range(1, owners):
        pl.semaphore_signal(barrier, inc=1, device_id=column_id(j), device_id_type=MESH)
    for j in range(1, pairs):
        pl.semaphore_signal(barrier, inc=1, device_id=pair_id(j), device_id_type=MESH)
    for j in range(1, chips):
        pl.semaphore_signal(barrier, inc=1, device_id=chip_id(j), device_id_type=MESH)

    def cols(h):
        return slice(h * D, (h + 1) * D)

    base_of = [sum(pieces[:g]) * owners for g in range(len(groups))]
    slot_of = [sum(pieces[:g]) for g in range(len(groups))]

    def rows_of(g, index):
        return pl.ds(pl.multiple_of(base_of[g] + index * pieces[g], 16), pieces[g])

    def slot(g):
        return pl.ds(slot_of[g], pieces[g])

    def phi(raw):
        low = jnp.exp(jnp.minimum(raw, 0.0))
        return jnp.where(raw > 0, raw + 1.0, low), jnp.where(raw > 0, 1.0, low)

    def rs_copy(p, g, j):
        dest = lax.rem(me + j, owners)
        return pltpu.make_async_remote_copy(
            src_ref=send_buf.at[p, rows_of(g, dest)],
            dst_ref=rs_buf.at[p, j, slot(g)],
            send_sem=rs_ssem.at[p, g, j], recv_sem=rs_rsem.at[p, g, j],
            device_id=column_id(j), device_id_type=MESH)

    def both(g):
        return pl.ds(2 * slot_of[g], 2 * pieces[g])

    def zh_copy(p, g, j):
        return pltpu.make_async_remote_copy(
            src_ref=zh_send.at[p, both(g)], dst_ref=zh_buf.at[p, j, both(g)],
            send_sem=zh_ssem.at[p, g, j], recv_sem=zh_rsem.at[p, g, j],
            device_id=pair_id(j), device_id_type=MESH)

    def fr_copy(p, g, j):
        return pltpu.make_async_remote_copy(
            src_ref=fr_send.at[p, slot(g)], dst_ref=fr_buf.at[p, j, slot(g)],
            send_sem=fr_ssem.at[p, g, j], recv_sem=fr_rsem.at[p, g, j],
            device_id=chip_id(j), device_id_type=MESH)

    def ag_copy(p, g, j):
        return pltpu.make_async_remote_copy(
            src_ref=ag_send.at[p, j % 2, slot(g)],
            dst_ref=whole.at[p, rows_of(g, me)],
            send_sem=ag_ssem.at[p, g, j], recv_sem=ag_rsem.at[p, g, j],
            device_id=column_id(j), device_id_type=MESH)

    def ag_wait(p, g, j):
        src = lax.rem(me - j + owners, owners)
        pltpu.make_async_remote_copy(
            src_ref=ag_send.at[p, j % 2, slot(g)],
            dst_ref=whole.at[p, rows_of(g, src)],
            send_sem=ag_ssem.at[p, g, j], recv_sem=ag_rsem.at[p, g, j],
            device_id=column_id(j), device_id_type=MESH).wait_recv()

    def start_rs(p, g):
        for j in range(1, owners):
            rs_copy(p, g, j).start()

    def reduce_rows(p, g):
        mine = send_buf[p, rows_of(g, me), :].astype(jnp.float32)
        other = None
        for j in range(1, owners):
            rs_copy(p, g, j).wait_recv()
        for j in range(1, owners):
            block = rs_buf[p, j, slot(g), :].astype(jnp.float32)
            if j % 2 == 0:
                mine = mine + block
            else:
                other = block if other is None else other + block
        share[p, 0, slot(g), :] = mine
        share[p, 1, slot(g), :] = other
        zh_send[p, both(g), :] = jnp.concatenate([mine, other], axis=0).astype(jnp.bfloat16)
        for j in range(1, pairs):
            zh_copy(p, g, j).start()

    def reduce_pairs(p, g):
        for j in range(1, pairs):
            zh_copy(p, g, j).wait_recv()
        mine, other = share[p, 0, slot(g), :], share[p, 1, slot(g), :]
        for j in range(1, pairs):
            block = zh_buf[p, j, both(g), :].astype(jnp.float32)
            mine = mine + block[:pieces[g]]
            other = other + block[pieces[g]:]
        share[p, 0, slot(g), :] = mine
        share[p, 1, slot(g), :] = other
        fr_send[p, slot(g), :] = (mine + other).astype(jnp.bfloat16)
        for j in range(1, chips):
            fr_copy(p, g, j).start()

    def scan_frames(p, g):
        for j in range(1, chips):
            fr_copy(p, g, j).wait_recv()
        base = jnp.zeros((pieces[g], LANES), jnp.float32)
        for j in range(1, chips):
            keep = (j <= chip) if p == 0 else (j > chip)
            base = base + jnp.where(keep, fr_buf[p, j, slot(g), :].astype(jnp.float32), 0.0)
        mine, other = share[p, 0, slot(g), :], share[p, 1, slot(g), :]
        own_last = (core == 1) if p == 0 else (core == 0)
        ag_send[p, 0, slot(g), :] = (base + mine + jnp.where(own_last, other, 0.0)).astype(jnp.bfloat16)
        ag_send[p, 1, slot(g), :] = (base + other + jnp.where(own_last, 0.0, mine)).astype(jnp.bfloat16)
        for j in range(1, owners):
            ag_copy(p, g, j).start()
        whole[p, rows_of(g, me), :] = ag_send[p, 0, slot(g), :]

    def wait_whole(p, g):
        for j in range(1, owners):
            ag_wait(p, g, j)

    span = range(len(groups))

    def head_state(p, g, i):
        return whole[p, base_of[g] + i * D:base_of[g] + (i + 1) * D, :D]

    loads[0].wait()
    loads[1].wait()
    for g in span:
        for i, h in enumerate(groups[g]):
            feat, slope = phi(k_raw[cols(h), :].astype(jnp.float32))
            feat = feat.astype(jnp.bfloat16)
            val = v_raw[cols(h), :]
            k_feat[h] = feat
            k_slope[h] = slope
            send_buf[0, base_of[g] + i * D:base_of[g] + (i + 1) * D, :D] = dot(feat, val, NT).astype(jnp.bfloat16)
        if g == 0:
            pl.semaphore_wait(barrier, owners - 1 + pairs - 1 + chips - 1)
        start_rs(0, g)

    loads[2].wait()
    loads[3].wait()
    tok, width = q_raw.shape[1], q_raw.shape[0]
    gain[...] = jnp.broadcast_to(gain_ref[...].reshape(1, width), (tok, width)).T
    for g in span:
        for h in groups[g]:
            feat, slope = phi(q_raw[cols(h), :].astype(jnp.float32))
            q_feat[h] = feat.astype(jnp.bfloat16)
            q_slope[h] = slope
            weighted[h] = g_raw[cols(h), :].astype(jnp.float32) * gain[cols(h), :]

    def store(src, dst, g, at):
        rows = pl.ds(groups[g][0] * D, len(groups[g]) * D)
        return pltpu.make_async_copy(src.at[rows], dst.at[rows], out_sem.at[at, g])

    stores = [
        [store(src, dst, g, at) for g in range(len(groups))]
        for at, (src, dst) in enumerate([(gq_out, gq_hbm), (gk_out, gk_hbm), (gv_out, gv_hbm)])
    ]

    def query_side(g):
        wait_whole(0, g)
        for i, h in enumerate(groups[g]):
            att = dot(head_state(0, g, i), q_feat[h], TN)
            w = weighted[h]
            inv = lax.rsqrt(jnp.mean(att * att, axis=0, keepdims=True) + 1e-6)
            inner = jnp.mean(w * att, axis=0, keepdims=True)
            ga = (inv * w - att * (inv * inv * inv * inner)).astype(jnp.bfloat16)
            grad_att[h] = ga
            row0 = base_of[g] + i * D
            send_buf[1, row0:row0 + D, :D] = dot(q_feat[h], ga, NT).astype(jnp.bfloat16)
        start_rs(1, g)

    def grad_query(g):
        for i, h in enumerate(groups[g]):
            gq = dot(head_state(0, g, i), grad_att[h], NN) * q_slope[h]
            gq_out[cols(h), :] = gq.astype(jnp.bfloat16)
        stores[0][g].start()

    def key_side(g):
        wait_whole(1, g)
        for i, h in enumerate(groups[g]):
            adj = head_state(1, g, i)
            gv_out[cols(h), :] = dot(adj, k_feat[h], TN).astype(jnp.bfloat16)
            gk_out[cols(h), :] = (dot(adj, v_raw[cols(h), :], NN) * k_slope[h]).astype(jnp.bfloat16)
        stores[1][g].start()
        stores[2][g].start()

    def staged(p, last, beside):
        for stage in (reduce_rows, reduce_pairs, scan_frames):
            for g in span:
                stage(p, g)
            if beside is not None and stage is not scan_frames:
                for g in span:
                    if (g == 0) == (stage is reduce_rows):
                        beside(g)
        for g in span:
            last(g)

    staged(0, query_side, None)
    staged(1, key_side, grad_query)

    for p in range(2):
        for g in span:
            for j in range(1, owners):
                rs_copy(p, g, j).wait_send()
                ag_copy(p, g, j).wait_send()
            for j in range(1, pairs):
                zh_copy(p, g, j).wait_send()
            for j in range(1, chips):
                fr_copy(p, g, j).wait_send()
    for c in sum(stores, []):
        c.wait()


def body(rows_n, frames_n, query_raw, key_raw, values, norm_gain, grad_out):
    tok, width = query_raw.shape
    heads = width // HEAD_DIM
    owners, pairs, chips = OWNERS, rows_n // 2, frames_n // 2
    groups = [list(range(s, min(s + GROUP, heads))) for s in range(0, heads, GROUP)]
    n = len(groups)
    unit = 16 * owners
    pieces = [-(-len(g) * HEAD_DIM // unit) * 16 for g in groups]
    piece = sum(pieces)
    bf, f32 = jnp.bfloat16, jnp.float32
    raw = pltpu.VMEM((width, tok), bf)
    per_head = lambda t: pltpu.VMEM((heads, HEAD_DIM, tok), t)
    dma = pltpu.SemaphoreType.DMA
    out = jax.ShapeDtypeStruct((width, tok), bf)
    flops = 12 * tok * heads * HEAD_DIM * HEAD_DIM
    hbm = pl.BlockSpec(memory_space=pl.ANY)
    grads = pl.pallas_call(
        functools.partial(kernel, groups, pieces, rows_n, frames_n),
        out_shape=(out, out, out),
        in_specs=[hbm, hbm, hbm, pl.BlockSpec(memory_space=pltpu.VMEM), hbm],
        out_specs=(hbm, hbm, hbm),
        scratch_shapes=[
            raw, raw, raw, raw, raw, raw, raw,
            per_head(bf), per_head(bf), pltpu.VMEM((width, tok), f32),
            per_head(f32), per_head(f32), per_head(f32), per_head(bf),
            pltpu.VMEM((2, owners * piece, LANES), bf),
            pltpu.VMEM((2, owners, piece, LANES), bf),
            pltpu.VMEM((2, 2, piece, LANES), f32),
            pltpu.VMEM((2, 2 * piece, LANES), bf),
            pltpu.VMEM((2, pairs, 2 * piece, LANES), bf),
            pltpu.VMEM((2, piece, LANES), bf),
            pltpu.VMEM((2, chips, piece, LANES), bf),
            pltpu.VMEM((2, 2, piece, LANES), bf),
            pltpu.VMEM((2, owners * piece, LANES), bf),
            dma((4,)), dma((3, n)),
            dma((2, n, owners)), dma((2, n, owners)),
            dma((2, n, pairs)), dma((2, n, pairs)),
            dma((2, n, chips)), dma((2, n, chips)),
            dma((2, n, owners)), dma((2, n, owners)),
        ],
        cost_estimate=pl.CostEstimate(
            flops=flops, bytes_accessed=14 * tok * width, transcendentals=2 * tok * width),
        compiler_params=pltpu.CompilerParams(
            collective_id=0, has_side_effects=True, vmem_limit_bytes=60 * 1024 * 1024),
    )(query_raw.T, key_raw.T, values.T, norm_gain, grad_out.T)
    return tuple(g.T for g in grads)


def solution(mesh):
    split = P(("frame", "row"), None)
    return jax.shard_map(
        functools.partial(body, mesh.shape["row"], mesh.shape["frame"]),
        mesh=mesh,
        in_specs=(split, split, split, P(), split),
        out_specs=(split, split, split),
        check_vma=False,
    )
```
